512 devices in a mesh: wide: 64 (over z, y), col: 8 (over x, core).
Axes of the slice: x: 4, y: 4, z: 16, core: 2. Of those that a mesh axis runs over, the one named last changes fastest.
Arguments:
- inputs: bfloat16 [1024, 6144], P('wide', 'col'), may hold values from -6 to 6
- out_grad: bfloat16 [1024, 6144], P('wide', 'col'), may hold values from -6 to 6
- preact: bfloat16 [1024, 24576], P('col', 'wide'), may hold values from -6 to 6
- w_in: bfloat16 [6144, 24576], P('col', 'wide'), may hold values from -0.078125 to 0.078125
- w_out: bfloat16 [24576, 6144], P('wide', 'col'), may hold values from -0.0390625 to 0.0390625
Outputs:
- in_grad: bfloat16 [1024, 6144], P('wide', 'col')
- w_in_grad: float32 [6144, 24576], P('col', 'wide')
- w_out_grad: float32 [24576, 6144], P('wide', 'col')
The draws below stay inside these ranges and needn't reach their ends.
All inputs are finite; a program needn't handle non-finite values.
Results may differ from the reference program's by a relative error of at most 0.02.
Values may be sent and summed in bfloat16 or wider, within the bound.
A program may use at most 64 MiB of HBM per device.

```python
import math
import jax
import jax.numpy as jnp
from jax import lax

D = 6144
FF = 24576
TOKENS = 1024
N_COL = 8


def level_of(key, shape, shards, low, high):
    level, own = 1.0, jax.random.fold_in(key, 6)
    for dim, shards_of in shards:
        draws = jnp.exp(jax.random.uniform(jax.random.fold_in(own, dim), (shards_of,), jnp.float32, low / len(shards), high / len(shards)))
        level = level * jnp.repeat(draws, shape[dim] // shards_of).reshape([-1 if axis == dim else 1 for axis in range(len(shape))])
    return level


def noise(key, shape, width, reach, split=(), dtype=jnp.bfloat16):
    values = width * jax.random.normal(key, shape, jnp.float32)
    if split:
        values = values * level_of(key, shape, split, -0.22, 0.18)
    return jnp.clip(values, -reach, reach).astype(dtype)


def setup_inputs(seed: int = 0) -> dict:
    keys = jax.random.split(jax.random.key(seed), 6)
    inputs = noise(keys[0], (TOKENS, D), 1.0, 6.0, ((0, 64), (1, 8)))
    out_grad = noise(keys[1], (TOKENS, D), 1.0, 6.0, ((0, 64), (1, 8)))
    preact = noise(keys[2], (TOKENS, FF), 1.0, 6.0, ((0, 8), (1, 64)))
    w_in = noise(keys[3], (D, FF), D ** -0.5, 0.078125, ((0, 8), (1, 64)))
    w_out = noise(keys[4], (FF, D), FF ** -0.5, 0.0390625, ((0, 64), (1, 8)))
    return {"inputs": inputs, "out_grad": out_grad, "preact": preact, "w_in": w_in, "w_out": w_out}


def gelu_grad(values):
    normal_cdf = 0.5 * (1.0 + lax.erf(values * (1.0 / math.sqrt(2.0))))
    density = jnp.exp(-0.5 * values * values) * (1.0 / math.sqrt(2.0 * math.pi))
    return normal_cdf + values * density

def reference(inputs, out_grad, preact, w_in, w_out):
    pre_float = preact.astype(jnp.float32)
    act = jax.nn.gelu(pre_float, approximate=False).astype(jnp.bfloat16)
    width_block = D // N_COL
    act_grad = jnp.zeros((TOKENS, FF), jnp.float32)
    for index in range(N_COL):
        grad_block = out_grad[:, index * width_block:(index + 1) * width_block]
        weight_block = w_out[:, index * width_block:(index + 1) * width_block]
        partial_sum = jnp.dot(grad_block, weight_block.T, preferred_element_type=jnp.float32)
        partial_sum = lax.optimization_barrier(partial_sum.astype(jnp.bfloat16))
        act_grad = act_grad + partial_sum.astype(jnp.float32)
    hidden_grad = (act_grad * gelu_grad(pre_float)).astype(jnp.bfloat16)
    w_out_grad = jnp.dot(act.T, out_grad, preferred_element_type=jnp.float32)
    w_in_grad = jnp.dot(inputs.T, hidden_grad, preferred_element_type=jnp.float32)
    in_grad = jnp.dot(hidden_grad, w_in.T, preferred_element_type=jnp.float32).astype(jnp.bfloat16)
    return (in_grad, w_in_grad, w_out_grad)
```

```python
import functools
import math

import jax
import jax.numpy as jnp
from jax import lax
from jax.experimental import pallas as pl
from jax.experimental.pallas import tpu as pltpu
from jax.sharding import PartitionSpec as P

MESH = pl.DeviceIdType.MESH
NZ, NY, NC = 16, 4, 8
ROWS = 16
STAGES = 4
BF16, F32 = jnp.bfloat16, jnp.float32


def normal_cdf(values):
    return 0.5 * (1.0 + lax.erf(values * (1.0 / math.sqrt(2.0))))


def gelu_grad(values):
    density = jnp.exp(-0.5 * values * values) * (1.0 / math.sqrt(2.0 * math.pi))
    return normal_cdf(values) + values * density


def dot(a, b, contract):
    return lax.dot_general(a, b, (contract, ((), ())), preferred_element_type=F32)


def stage_offset(stage, quarter):
    return -(2 * stage + 1) + quarter % 2 + (4 * stage + 2) * (quarter // 2)


def slot_of(offset):
    return offset + 7


def back(offset):
    return 8 if offset == 8 else -offset


def kernel(
    grad_hbm, inp_hbm, pre_hbm, w_in_hbm, w_out_hbm,
    in_grad_ref, w_in_grad_hbm, w_out_grad_hbm,
    g, inp, pre, act, hid, w_in, w_out, xs, xr, part, ys, yr, zs, zr, wig, wog,
    local_sem,
    gz_s, gz_r, gy_s, gy_r, pre_s, pre_r, x_s, x_r, h_s, h_r, y_s, y_r, z_s, z_r, iy_s, iy_r, iz_s, iz_r,
):
    wide, col = lax.axis_index("wide"), lax.axis_index("col")
    z, y = wide // NY, wide % NY

    def at_z(offset):
        return (z + offset + NZ) % NZ

    def at_y(offset):
        return (y + offset) % NY

    def dev_z(offset):
        return (at_z(offset) * NY + y, col)

    def dev_y(offset):
        return (z * NY + at_y(offset), col)

    def dev_c(offset):
        return (wide, (col + offset) % NC)

    sends = []

    def send(src, dst, send_sem, recv_sem, device):
        copy = pltpu.make_async_remote_copy(
            src_ref=src, dst_ref=dst, send_sem=send_sem, recv_sem=recv_sem, device_id=device, device_id_type=MESH
        )
        copy.start()
        sends.append(copy)

    def arrived(dst, send_sem, recv_sem):
        pltpu.make_async_remote_copy(
            src_ref=dst, dst_ref=dst, send_sem=send_sem, recv_sem=recv_sem, device_id=dev_y(1), device_id_type=MESH
        ).wait_recv()

    loads = [
        pltpu.make_async_copy(grad_hbm, g.at[z, y], local_sem.at[0]),
        pltpu.make_async_copy(pre_hbm, pre.at[pl.ds(2 * col, 2)], local_sem.at[1]),
        pltpu.make_async_copy(inp_hbm, inp.at[z, y], local_sem.at[2]),
        pltpu.make_async_copy(w_out_hbm, w_out, local_sem.at[3]),
        pltpu.make_async_copy(w_in_hbm, w_in, local_sem.at[4]),
    ]
    for load in loads:
        load.start()

    barrier = pltpu.get_barrier_semaphore()
    partners = [dev_z(d) for d in (1, -1, 2, -2)] + [dev_y(d) for d in (1, 2, 3)] + [dev_c(d) for d in range(1, NC)]
    for partner in partners:
        pl.semaphore_signal(barrier, inc=1, device_id=partner, device_id_type=MESH)
    pl.semaphore_wait(barrier, len(partners))

    def z_pass(offset, hop):
        seen = offset - hop
        block = g.at[at_z(offset), y]
        send(block, block, gz_s.at[slot_of(seen)], gz_r.at[slot_of(seen)], dev_z(hop))

    def z_wait(offset):
        arrived(g.at[at_z(offset), y], gz_s.at[slot_of(offset)], gz_r.at[slot_of(offset)])

    def y_pass(offset):
        block = g.at[at_z(offset), y]
        for d in (1, 2, 3):
            send(block, block, gy_s.at[slot_of(offset), d - 1], gy_r.at[slot_of(offset), d - 1], dev_y(d))

    def y_wait(offset):
        for d in (1, 2, 3):
            arrived(
                g.at[at_z(offset), at_y(NY - d)], gy_s.at[slot_of(offset), d - 1], gy_r.at[slot_of(offset), d - 1]
            )

    def gather_step(step):
        far, near = 2 * step + 2, 2 * step + 1
        z_wait(far)
        if step < 3:
            z_pass(far, -2)
            z_pass(far, -1)
            z_wait(-far)
            if step < 2:
                z_pass(-far, 2)
            z_pass(-far, 1)
        y_pass(far)
        if step < 3:
            y_pass(-far)
        z_wait(near)
        y_pass(near)
        z_wait(-near)
        y_pass(-near)

    def inputs_over_y():
        block = inp.at[z, y]
        for d in (1, 2, 3):
            send(block, block, iy_s.at[d - 1], iy_r.at[d - 1], dev_y(d))

    def inputs_step(step):
        if step == 0:
            for d in (1, 2, 3):
                arrived(inp.at[z, at_y(NY - d)], iy_s.at[d - 1], iy_r.at[d - 1])
        for way in (1, -1):
            offset = way * step
            if step and offset != -8:
                arrived(inp.at[at_z(offset)], iz_s.at[slot_of(offset)], iz_r.at[slot_of(offset)])
            seen = offset + way
            if step < 8 and seen != -8:
                block = inp.at[at_z(offset)]
                send(block, block, iz_s.at[slot_of(seen)], iz_r.at[slot_of(seen)], dev_z(-way))

    def gelu_chunk(index):
        values = pre[pl.ds(2 * index, 2)].astype(F32)
        act[pl.ds(2 * index, 2)] = (values * normal_cdf(values)).astype(BF16)

    def stage_blocks(stage):
        return [at_z(stage_offset(stage, quarter)) for quarter in range(4)]

    def stage_rows(ref, stage):
        return jnp.concatenate([ref[b].reshape(NY * ROWS, ref.shape[-1]) for b in stage_blocks(stage)], axis=0)

    own_block = [at_z(stage_offset(stage, col // 2)) for stage in range(STAGES)]
    own_half = pl.ds(2 * (col % 2), 2)

    def phase_b(stage):
        for quarter in range(4):
            y_wait_offset = stage_offset(stage, quarter)
            y_wait(y_wait_offset)
        partial = dot(stage_rows(g, stage), w_out[...], ((1,), (1,))).astype(BF16)
        xs[stage] = partial.reshape(NC, 2, ROWS, partial.shape[-1])
        for r in range(1, NC):
            send(xs.at[stage, (col + r) % NC], xr.at[stage, r], x_s.at[stage, r], x_r.at[stage, r], dev_c(r))

    def phase_c(stage):
        total = xs[stage, col].astype(F32)
        for r in range(1, NC):
            arrived(xr.at[stage, r], x_s.at[stage, r], x_r.at[stage, r])
            total = total + xr[stage, r].astype(F32)
        block = own_block[stage]
        own = pre[block, own_half].astype(F32)
        hid[block, own_half] = (total * gelu_grad(own)).astype(BF16)
        piece = hid.at[block, own_half]
        for r in range(1, NC):
            send(piece, piece, h_s.at[stage, r], h_r.at[stage, r], dev_c(r))

    def phase_d(stage):
        for r in range(1, NC):
            source = (col + NC - r) % NC
            piece = hid.at[at_z(stage_offset(stage, source // 2)), pl.ds(2 * (source % 2), 2)]
            arrived(piece, h_s.at[stage, r], h_r.at[stage, r])
        partial = dot(stage_rows(hid, stage), w_in[...], ((1,), (1,)))
        part[stage] = partial.reshape(4, NY, ROWS, partial.shape[-1])
        for d in (2, 1, 3):
            ys[stage, d - 1] = part[stage, :, at_y(d)].astype(BF16)
            send(ys.at[stage, d - 1], yr.at[stage, d - 1], y_s.at[stage, d - 1], y_r.at[stage, d - 1], dev_y(d))

    def phase_e(stage):
        for d in (1, 2, 3):
            arrived(yr.at[stage, d - 1], y_s.at[stage, d - 1], y_r.at[stage, d - 1])
        for quarter in (3, 0, 2, 1):
            offset = stage_offset(stage, quarter)
            total = part[stage, quarter, y]
            for d in (1, 2, 3):
                total = total + yr[stage, d - 1, quarter].astype(F32)
            seen = slot_of(back(offset))
            zs[seen] = total.astype(BF16)
            if offset:
                send(zs.at[seen], zr.at[seen], z_s.at[seen], z_r.at[seen], dev_z(offset))

    loads[0].wait()
    for hop in (2, -2, 1, -1):
        z_pass(0, hop)
    y_pass(0)
    loads[1].wait()
    own_pre = pre.at[pl.ds(2 * col, 2)]
    for r in range(1, NC):
        send(own_pre, own_pre, pre_s.at[r], pre_r.at[r], dev_c(r))
    loads[2].wait()
    inputs_over_y()
    loads[3].wait()
    loads[4].wait()

    stores = []
    for it in range(2 * STAGES):
        if it < STAGES:
            gather_step(it)
        inputs_step(it)
        for phase, lag in ((phase_b, 1), (phase_c, 2), (phase_d, 3), (phase_e, 4)):
            if 0 <= it - lag < STAGES:
                phase(it - lag)
        if it == 0:
            for r in range(1, NC):
                arrived(pre.at[pl.ds(2 * ((col + NC - r) % NC), 2)], pre_s.at[r], pre_r.at[r])
        if it < 4:
            gelu_chunk(2 * it)
            gelu_chunk(2 * it + 1)
        if it == 4:
            wog[...] = dot(
                act[...].reshape(NZ * NY * ROWS, act.shape[-1]), g[...].reshape(NZ * NY * ROWS, g.shape[-1]), ((0,), (0,))
            )
            store = pltpu.make_async_copy(wog, w_out_grad_hbm, local_sem.at[5])
            store.start()
            stores.append(store)
    inputs_step(8)
    wig[...] = dot(
        inp[...].reshape(NZ * NY * ROWS, inp.shape[-1]), hid[...].reshape(NZ * NY * ROWS, hid.shape[-1]), ((0,), (0,))
    )
    store = pltpu.make_async_copy(wig, w_in_grad_hbm, local_sem.at[6])
    store.start()
    stores.append(store)

    total = zs[slot_of(0)].astype(F32)
    for offset in (1, -1, 2, -2, 3, -3, 4, -4, 5, -5, 6, -6, 7, -7, 8):
        seen = slot_of(offset)
        arrived(zr.at[seen], z_s.at[seen], z_r.at[seen])
        total = total + zr[seen].astype(F32)
    in_grad_ref[...] = total.astype(BF16)
    for copy in sends:
        copy.wait_send()
    for store in stores:
        store.wait()


def body(inputs, out_grad, preact, w_in, w_out):
    width, hidden = w_in.shape
    dma = pltpu.SemaphoreType.DMA
    any_space = pl.BlockSpec(memory_space=pl.ANY)
    pairs = [(16,), (16, 3), (NC,), (STAGES, NC), (STAGES, NC), (STAGES, 3), (16,), (3,), (16,)]
    return pl.pallas_call(
        kernel,
        name="mlp_backward",
        out_shape=(
            jax.ShapeDtypeStruct((ROWS, width), BF16),
            jax.ShapeDtypeStruct((width, hidden), F32),
            jax.ShapeDtypeStruct((hidden, width), F32),
        ),
        in_specs=[any_space] * 5,
        out_specs=(pl.BlockSpec(memory_space=pltpu.VMEM), any_space, any_space),
        scratch_shapes=[
            pltpu.VMEM((NZ, NY, ROWS, width), BF16),
            pltpu.VMEM((NZ, NY, ROWS, width), BF16),
            pltpu.VMEM((NZ, NY, ROWS, hidden), BF16),
            pltpu.VMEM((NZ, NY, ROWS, hidden), BF16),
            pltpu.VMEM((NZ, NY, ROWS, hidden), BF16),
            pltpu.VMEM((width, hidden), BF16),
            pltpu.VMEM((hidden, width), BF16),
            pltpu.VMEM((STAGES, NC, 2, ROWS, hidden), BF16),
            pltpu.VMEM((STAGES, NC, 2, ROWS, hidden), BF16),
            pltpu.VMEM((STAGES, 4, NY, ROWS, width), F32),
            pltpu.VMEM((STAGES, 3, 4, ROWS, width), BF16),
            pltpu.VMEM((STAGES, 3, 4, ROWS, width), BF16),
            pltpu.VMEM((16, ROWS, width), BF16),
            pltpu.VMEM((16, ROWS, width), BF16),
            pltpu.VMEM((width, hidden), F32),
            pltpu.VMEM((hidden, width), F32),
            dma((7,)),
        ]
        + [dma(shape) for shape in pairs for _ in range(2)],
        compiler_params=pltpu.CompilerParams(collective_id=0, has_side_effects=True, vmem_limit_bytes=48 << 20),
    )(out_grad, inputs, preact.reshape(2, NY, ROWS, hidden), w_in, w_out)


def solution(mesh):
    placed = (
        P("wide", "col"),
        P("wide", "col"),
        P("col", "wide"),
        P("col", "wide"),
        P("wide", "col"),
    )
    return jax.shard_map(
        body,
        mesh=mesh,
        in_specs=placed,
        out_specs=(P("wide", "col"), P("col", "wide"), P("wide", "col")),
        check_vma=False,
    )
```

```python
import functools
import math

import jax
import jax.numpy as jnp
from jax import lax
from jax.experimental import pallas as pl
from jax.experimental.pallas import tpu as pltpu
from jax.sharding import PartitionSpec as P

MESH = pl.DeviceIdType.MESH
NZ, NY, NC = 16, 4, 8
ROWS = 16
HEAD = 256
INP_HEAD = 256
INP_REACH = 2
STAGES = 4
BF16, F32 = jnp.bfloat16, jnp.float32


def normal_cdf(values):
    return 0.5 * (1.0 + lax.erf(values * (1.0 / math.sqrt(2.0))))


def gelu_grad(values):
    density = jnp.exp(-0.5 * values * values) * (1.0 / math.sqrt(2.0 * math.pi))
    return normal_cdf(values) + values * density


def dot(a, b, contract):
    return lax.dot_general(a, b, (contract, ((), ())), preferred_element_type=F32)


def stage_offset(stage, quarter):
    return -(2 * stage + 1) + quarter % 2 + (4 * stage + 2) * (quarter // 2)


def slot_of(offset):
    return offset + 7


def back(offset):
    return 8 if offset == 8 else -offset


def kernel(
    grad_hbm, inp_hbm, pre_hbm, w_in_hbm, w_out_hbm,
    in_grad_ref, wig, wog,
    ga, gb, ia, ib, pre, act, hid, w_in, w_out, xs, xr, part, ys, yr, zs, zr,
    local_sem,
    grad_sems, inp_sems, pre_s, pre_r, x_s, x_r, h_s, h_r, y_s, y_r, z_s, z_r,
):
    wide, col = lax.axis_index("wide"), lax.axis_index("col")
    z, y, x, core = wide // NY, wide % NY, col // 2, col % 2

    def at_z(offset):
        return (z + offset + NZ) % NZ

    def at_y(offset):
        return (y + offset) % NY

    def dev_z(offset):
        return (at_z(offset) * NY + y, col)

    def dev_y(offset):
        return (z * NY + at_y(offset), col)

    col_offsets = (4, 5, 2, 3, 6, 7, 1)

    def other_col(offset):
        return 2 * ((x + offset // 2) % 4) + (core + offset) % 2

    def dev_c(offset):
        return (wide, other_col(offset))

    def source_col(offset):
        return 2 * ((x + 4 - offset // 2) % 4) + (core + offset) % 2

    sends = []

    def send(src, dst, send_sem, recv_sem, device):
        copy = pltpu.make_async_remote_copy(
            src_ref=src, dst_ref=dst, send_sem=send_sem, recv_sem=recv_sem, device_id=device, device_id_type=MESH
        )
        copy.start()
        sends.append(copy)

    def arrived(dst, send_sem, recv_sem):
        pltpu.make_async_remote_copy(
            src_ref=dst, dst_ref=dst, send_sem=send_sem, recv_sem=recv_sem, device_id=dev_y(1), device_id_type=MESH
        ).wait_recv()

    def local(src, dst, index):
        copy = pltpu.make_async_copy(src, dst, local_sem.at[index])
        copy.start()
        return copy

    grad_loads = [
        local(grad_hbm.at[:, HEAD:], gb.at[z, y], 0),
        local(grad_hbm.at[:, :HEAD], ga.at[z, y], 1),
    ]
    pre_load = local(pre_hbm, pre.at[pl.ds(2 * col, 2)], 2)
    inp_loads = [local(inp_hbm.at[:, INP_HEAD:], ib.at[z, y], 3)] if INP_HEAD < inp_hbm.shape[1] else []
    inp_loads.append(local(inp_hbm.at[:, :INP_HEAD], ia.at[z, y], 6))

    barrier = pltpu.get_barrier_semaphore()
    greeted = [dev_z(d) for d in (1, -1, 2, -2)] + [dev_y(d) for d in (1, 2, 3)] + [dev_c(r) for r in col_offsets]
    for other in greeted:
        pl.semaphore_signal(barrier, inc=1, device_id=other, device_id_type=MESH)
    pl.semaphore_wait(barrier, len(greeted))

    def gather(head, rest, sems, reach):
        hy_s, hy_r, hz_s, hz_r, rz_s, rz_r, ry_s, ry_r = sems

        def head_block(offset):
            return head.at[at_z(offset)], hz_s, hz_r

        def rest_block(offset):
            return rest.at[at_z(offset), y], rz_s, rz_r

        def z_pass(part, offset, hop):
            seen = slot_of(offset - hop)
            block, send_sem, recv_sem = part(offset)
            send(block, block, send_sem.at[seen], recv_sem.at[seen], dev_z(hop))

        def z_wait(part, offset):
            block, send_sem, recv_sem = part(offset)
            arrived(block, send_sem.at[slot_of(offset)], recv_sem.at[slot_of(offset)])

        def y_pass(offset):
            block = rest.at[at_z(offset), y]
            for d in (1, 3, 2):
                slot = NY * slot_of(offset) + d
                send(block, block, ry_s.at[slot], ry_r.at[slot], dev_y(d))

        def y_wait(offset):
            for d in (1, 2, 3):
                slot = NY * slot_of(offset) + d
                arrived(rest.at[at_z(offset), at_y(NY - d)], ry_s.at[slot], ry_r.at[slot])

        def z_start(part):
            for hop in range(reach, 0, -1):
                z_pass(part, 0, hop)
                z_pass(part, 0, -hop)

        def z_step(part, step, then):
            waiting = []
            for back_off in range(reach):
                for way in (1, -1):
                    offset = way * (reach * step - back_off)
                    if offset == -8:
                        continue
                    z_wait(part, offset)
                    if back_off == 0 and reach * step < 8:
                        for hop in range(reach, 0, -1):
                            if offset + hop * way != -8:
                                z_pass(part, offset, -hop * way)
                    waiting.append(offset)
                    if back_off or way < 0 or reach * step == 8:
                        for passed in waiting:
                            then(passed)
                        waiting = []

        def start():
            if rest is not None:
                z_start(rest_block)
            block = head.at[z, y]
            for d in (1, 3, 2):
                send(block, block, hy_s.at[d], hy_r.at[d], dev_y(d))
            if rest is not None:
                y_pass(0)

        def rest_step(step):
            z_step(rest_block, step, y_pass)

        def head_step(step):
            if step == 0:
                for d in (1, 2, 3):
                    arrived(head.at[z, at_y(NY - d)], hy_s.at[d], hy_r.at[d])
                z_start(head_block)
            else:
                z_step(head_block, step, lambda offset: None)

        return start, rest_step, head_step, y_wait

    grad_start, grad_rest, grad_head, grad_wait = gather(ga, gb, grad_sems, 2)
    inp_start, inp_rest, inp_head, inp_wait = gather(ia, ib, inp_sems, INP_REACH)

    def flat(ref):
        return ref[...].reshape(NZ * NY * ROWS, ref.shape[-1])

    def gelu_chunk(index):
        values = pre[pl.ds(2 * index, 2)].astype(F32)
        act[pl.ds(2 * index, 2)] = (values * normal_cdf(values)).astype(BF16)

    def stage_blocks(stage):
        return [at_z(stage_offset(stage, quarter)) for quarter in range(4)]

    def stage_rows(ref, stage):
        return jnp.concatenate([ref[b].reshape(NY * ROWS, ref.shape[-1]) for b in stage_blocks(stage)], axis=0)

    own_block = [at_z(stage_offset(stage, col // 2)) for stage in range(STAGES)]
    own_half = pl.ds(2 * (col % 2), 2)

    def phase_b(stage):
        for quarter in range(4):
            grad_wait(stage_offset(stage, quarter))
        partial = dot(stage_rows(ga, stage), w_out[:, :HEAD], ((1,), (1,)))
        partial = (partial + dot(stage_rows(gb, stage), w_out[:, HEAD:], ((1,), (1,)))).astype(BF16)
        xs[stage] = partial.reshape(NC, 2, ROWS, partial.shape[-1])
        for r in col_offsets:
            send(xs.at[stage, other_col(r)], xr.at[stage, r], x_s.at[stage, r], x_r.at[stage, r], dev_c(r))

    def phase_c(stage):
        total = xs[stage, col].astype(F32)
        for r in col_offsets[::-1]:
            arrived(xr.at[stage, r], x_s.at[stage, r], x_r.at[stage, r])
            total = total + xr[stage, r].astype(F32)
        block = own_block[stage]
        own = pre[block, own_half].astype(F32)
        hid[block, own_half] = (total * gelu_grad(own)).astype(BF16)
        piece = hid.at[block, own_half]
        for r in col_offsets:
            send(piece, piece, h_s.at[stage, r], h_r.at[stage, r], dev_c(r))

    def phase_d(stage):
        for r in col_offsets[::-1]:
            source = source_col(r)
            piece = hid.at[at_z(stage_offset(stage, source // 2)), pl.ds(2 * (source % 2), 2)]
            arrived(piece, h_s.at[stage, r], h_r.at[stage, r])
        partial = dot(stage_rows(hid, stage), w_in[...], ((1,), (1,)))
        part[stage] = partial.reshape(4, NY, ROWS, partial.shape[-1])
        for quarter in (3, 0, 2, 1):
            for d in (2, 1, 3):
                slot = NY * quarter + d
                ys[stage, slot] = part[stage, quarter, at_y(d)].astype(BF16)
                send(ys.at[stage, slot], yr.at[stage, slot], y_s.at[stage, slot], y_r.at[stage, slot], dev_y(d))

    def phase_e(stage):
        for quarter in (3, 0, 2, 1):
            offset = stage_offset(stage, quarter)
            total = part[stage, quarter, y]
            for d in (1, 3, 2):
                slot = NY * quarter + d
                arrived(yr.at[stage, slot], y_s.at[stage, slot], y_r.at[stage, slot])
                total = total + yr[stage, slot].astype(F32)
            seen = slot_of(back(offset))
            zs[seen] = total.astype(BF16)
            if offset:
                send(zs.at[seen], zr.at[seen], z_s.at[seen], z_r.at[seen], dev_z(offset))

    for load in grad_loads:
        load.wait()
    grad_start()
    pre_load.wait()
    own_pre = pre.at[pl.ds(2 * col, 2)]
    for r in col_offsets:
        send(own_pre, own_pre, pre_s.at[r], pre_r.at[r], dev_c(r))
    weight_loads = [local(w_out_hbm, w_out, 4), local(w_in_hbm, w_in, 5)]

    def start_inputs():
        for load in inp_loads:
            load.wait()
        inp_start()

    def wait_preact():
        for r in col_offsets:
            arrived(pre.at[pl.ds(2 * source_col(r), 2)], pre_s.at[r], pre_r.at[r])

    def wait_weights():
        for load in weight_loads:
            load.wait()

    def gelu_part(index):
        gelu_chunk(2 * index)
        gelu_chunk(2 * index + 1)

    def w_out_grad():
        for gathered, columns in ((ga, slice(0, HEAD)), (gb, slice(HEAD, None))):
            wog[:, columns] = dot(flat(act), flat(gathered), ((0,), (0,)))

    def w_in_grad():
        if ib is not None:
            for offset in range(-7, 9):
                inp_wait(offset)
            wig[INP_HEAD:] = dot(flat(ib), flat(hid), ((0,), (0,)))
        wig[:INP_HEAD] = dot(flat(ia), flat(hid), ((0,), (0,)))

    for step, *index in (
        (grad_rest, 1), (grad_head, 0), (wait_weights,), (start_inputs,), (grad_rest, 2), (grad_head, 1),
        (inp_rest, 1), (inp_head, 0), (phase_b, 0), (wait_preact,), (gelu_part, 0), (gelu_part, 1), (grad_rest, 3),
        (grad_head, 2), (inp_rest, 2), (inp_head, 1), (phase_b, 1), (phase_c, 0), (gelu_part, 2), (gelu_part, 3),
        (grad_rest, 4), (grad_head, 3), (inp_rest, 3), (inp_head, 2), (phase_b, 2), (phase_c, 1), (phase_d, 0),
        (grad_head, 4), (phase_b, 3), (inp_rest, 4), (inp_head, 3), (phase_c, 2), (phase_d, 1), (phase_e, 0),
        (w_out_grad,), (phase_c, 3), (inp_head, 4), (phase_d, 2), (phase_e, 1), (phase_d, 3), (phase_e, 2),
        (phase_e, 3), (w_in_grad,),
    ):
        step(*index)

    total = zs[slot_of(0)].astype(F32)
    for offset in (1, -1, 2, -2, 3, -3, 4, -4, 5, -5, 6, -6, 7, -7, 8):
        seen = slot_of(offset)
        arrived(zr.at[seen], z_s.at[seen], z_r.at[seen])
        total = total + zr[seen].astype(F32)
    in_grad_ref[...] = total.astype(BF16)
    for copy in sends:
        copy.wait_send()


def body(inputs, out_grad, preact, w_in, w_out):
    width, hidden = w_in.shape
    dma = pltpu.SemaphoreType.DMA
    any_space = pl.BlockSpec(memory_space=pl.ANY)
    gather_sems = [dma((size,)) for size in (NY, NY, 16, 16, 16, 16, 16 * NY, 16 * NY)]
    pairs = [(NC,), (STAGES, NC), (STAGES, NC), (STAGES, 4 * NY), (16,)]
    return pl.pallas_call(
        kernel,
        name="mlp_backward",
        out_shape=(
            pltpu.VMEM((ROWS, width), BF16),
            pltpu.VMEM((width, hidden), F32),
            pltpu.VMEM((hidden, width), F32),
        ),
        in_specs=[any_space] * 5,
        out_specs=(pl.BlockSpec(memory_space=pltpu.VMEM),) * 3,
        scratch_shapes=[
            pltpu.VMEM((NZ, NY, ROWS, HEAD), BF16),
            pltpu.VMEM((NZ, NY, ROWS, width - HEAD), BF16),
            pltpu.VMEM((NZ, NY, ROWS, INP_HEAD), BF16),
            pltpu.VMEM((NZ, NY, ROWS, width - INP_HEAD), BF16) if INP_HEAD < width else None,
            pltpu.VMEM((NZ, NY, ROWS, hidden), BF16),
            pltpu.VMEM((NZ, NY, ROWS, hidden), BF16),
            pltpu.VMEM((NZ, NY, ROWS, hidden), BF16),
            pltpu.VMEM((width, hidden), BF16),
            pltpu.VMEM((hidden, width), BF16),
            pltpu.VMEM((STAGES, NC, 2, ROWS, hidden), BF16),
            pltpu.VMEM((STAGES, NC, 2, ROWS, hidden), BF16),
            pltpu.VMEM((STAGES, 4, NY, ROWS, width), F32),
            pltpu.VMEM((STAGES, 4 * NY, ROWS, width), BF16),
            pltpu.VMEM((STAGES, 4 * NY, ROWS, width), BF16),
            pltpu.VMEM((16, ROWS, width), BF16),
            pltpu.VMEM((16, ROWS, width), BF16),
            dma((7,)),
            gather_sems,
            gather_sems,
        ]
        + [dma(shape) for shape in pairs for _ in range(2)],
        compiler_params=pltpu.CompilerParams(collective_id=0, has_side_effects=True, vmem_limit_bytes=60 << 20),
    )(out_grad, inputs, preact.reshape(2, NY, ROWS, hidden), w_in, w_out)


def solution(mesh):
    placed = (
        P("wide", "col"),
        P("wide", "col"),
        P("col", "wide"),
        P("col", "wide"),
        P("wide", "col"),
    )
    return jax.shard_map(
        body,
        mesh=mesh,
        in_specs=placed,
        out_specs=(P("wide", "col"), P("col", "wide"), P("wide", "col")),
        check_vma=False,
    )
```

```python
import functools
import math

import jax
import jax.numpy as jnp
from jax import lax
from jax.experimental import pallas as pl
from jax.experimental.pallas import tpu as pltpu
from jax.sharding import PartitionSpec as P

MESH = pl.DeviceIdType.MESH
NZ, NY, NC = 16, 4, 8
ROWS = 16
HEAD = 256
INP_HEAD = 384
INP_REACH = 2
STAGES = 4
BF16, F32 = jnp.bfloat16, jnp.float32


def normal_cdf(values):
    return 0.5 * (1.0 + lax.erf(values * (1.0 / math.sqrt(2.0))))


def gelu_grad(values):
    density = jnp.exp(-0.5 * values * values) * (1.0 / math.sqrt(2.0 * math.pi))
    return normal_cdf(values) + values * density


def dot(a, b, contract):
    return lax.dot_general(a, b, (contract, ((), ())), preferred_element_type=F32)


def stage_offset(stage, quarter):
    return -(2 * stage + 1) + quarter % 2 + (4 * stage + 2) * (quarter // 2)


def slot_of(offset):
    return offset + 7


def back(offset):
    return 8 if offset == 8 else -offset


def kernel(
    grad_hbm, inp_hbm, pre_hbm, w_in_hbm, w_out_hbm,
    in_grad_ref, wig, wog,
    ga, gb, ia, ib, pre, act, hid, w_in, w_out, xs, xr, part, ys, yr, zs, zr,
    local_sem,
    grad_sems, inp_sems, pre_s, pre_r, x_s, x_r, h_s, h_r, y_s, y_r, z_s, z_r,
):
    wide, col = lax.axis_index("wide"), lax.axis_index("col")
    z, y, x, core = wide // NY, wide % NY, col // 2, col % 2

    def at_z(offset):
        return (z + offset + NZ) % NZ

    def at_y(offset):
        return (y + offset) % NY

    def dev_z(offset):
        return (at_z(offset) * NY + y, col)

    def dev_y(offset):
        return (z * NY + at_y(offset), col)

    col_offsets = (4, 5, 2, 3, 6, 7, 1)

    def other_col(offset):
        return 2 * ((x + offset // 2) % 4) + (core + offset) % 2

    def dev_c(offset):
        return (wide, other_col(offset))

    def source_col(offset):
        return 2 * ((x + 4 - offset // 2) % 4) + (core + offset) % 2

    sends = []

    def send(src, dst, send_sem, recv_sem, device):
        copy = pltpu.make_async_remote_copy(
            src_ref=src, dst_ref=dst, send_sem=send_sem, recv_sem=recv_sem, device_id=device, device_id_type=MESH
        )
        copy.start()
        sends.append(copy)

    def arrived(dst, send_sem, recv_sem):
        pltpu.make_async_remote_copy(
            src_ref=dst, dst_ref=dst, send_sem=send_sem, recv_sem=recv_sem, device_id=dev_y(1), device_id_type=MESH
        ).wait_recv()

    def local(src, dst, index):
        copy = pltpu.make_async_copy(src, dst, local_sem.at[index])
        copy.start()
        return copy

    grad_loads = [
        local(grad_hbm.at[:, HEAD:], gb.at[z, y], 0),
        local(grad_hbm.at[:, :HEAD], ga.at[z, y], 1),
    ]
    pre_load = local(pre_hbm, pre.at[pl.ds(2 * col, 2)], 2)
    inp_loads = [local(inp_hbm.at[:, INP_HEAD:], ib.at[z, y], 3)] if INP_HEAD < inp_hbm.shape[1] else []
    inp_loads.append(local(inp_hbm.at[:, :INP_HEAD], ia.at[z, y], 6))

    barrier = pltpu.get_barrier_semaphore()
    greeted = [dev_z(d) for d in (1, -1, 2, -2)] + [dev_y(d) for d in (1, 2, 3)] + [dev_c(r) for r in col_offsets]
    for other in greeted:
        pl.semaphore_signal(barrier, inc=1, device_id=other, device_id_type=MESH)
    pl.semaphore_wait(barrier, len(greeted))

    def gather(head, rest, sems, reach):
        hy_s, hy_r, hz_s, hz_r, rz_s, rz_r, ry_s, ry_r = sems

        def head_block(offset):
            return head.at[at_z(offset)], hz_s, hz_r

        def rest_block(offset):
            return rest.at[at_z(offset), y], rz_s, rz_r

        def z_pass(part, offset, hop):
            seen = slot_of(offset - hop)
            block, send_sem, recv_sem = part(offset)
            send(block, block, send_sem.at[seen], recv_sem.at[seen], dev_z(hop))

        def z_wait(part, offset):
            block, send_sem, recv_sem = part(offset)
            arrived(block, send_sem.at[slot_of(offset)], recv_sem.at[slot_of(offset)])

        def y_pass(offset):
            block = rest.at[at_z(offset), y]
            for d in (1, 3, 2):
                slot = NY * slot_of(offset) + d
                send(block, block, ry_s.at[slot], ry_r.at[slot], dev_y(d))

        def y_wait(offset):
            for d in (1, 2, 3):
                slot = NY * slot_of(offset) + d
                arrived(rest.at[at_z(offset), at_y(NY - d)], ry_s.at[slot], ry_r.at[slot])

        def z_start(part):
            for hop in range(reach, 0, -1):
                z_pass(part, 0, hop)
                z_pass(part, 0, -hop)

        def z_step(part, step, then):
            waiting = []
            for back_off in range(reach):
                for way in (1, -1):
                    offset = way * (reach * step - back_off)
                    if offset == -8:
                        continue
                    z_wait(part, offset)
                    if back_off == 0 and reach * step < 8:
                        for hop in range(reach, 0, -1):
                            if offset + hop * way != -8:
                                z_pass(part, offset, -hop * way)
                    waiting.append(offset)
                    if back_off or way < 0 or reach * step == 8:
                        for passed in waiting:
                            then(passed)
                        waiting = []

        def start():
            if rest is not None:
                z_start(rest_block)
            block = head.at[z, y]
            for d in (1, 3, 2):
                send(block, block, hy_s.at[d], hy_r.at[d], dev_y(d))
            if rest is not None:
                y_pass(0)

        def rest_step(step):
            z_step(rest_block, step, y_pass)

        def head_step(step):
            if step == 0:
                for d in (1, 2, 3):
                    arrived(head.at[z, at_y(NY - d)], hy_s.at[d], hy_r.at[d])
                z_start(head_block)
            else:
                z_step(head_block, step, lambda offset: None)

        return start, rest_step, head_step, y_wait

    grad_start, grad_rest, grad_head, grad_wait = gather(ga, gb, grad_sems, 2)
    inp_start, inp_rest, inp_head, inp_wait = gather(ia, ib, inp_sems, INP_REACH)

    def flat(ref):
        return ref[...].reshape(NZ * NY * ROWS, ref.shape[-1])

    def gelu_chunk(index):
        values = pre[pl.ds(2 * index, 2)].astype(F32)
        act[pl.ds(2 * index, 2)] = (values * normal_cdf(values)).astype(BF16)

    def stage_blocks(stage):
        return [at_z(stage_offset(stage, quarter)) for quarter in range(4)]

    def stage_rows(ref, stage):
        return jnp.concatenate([ref[b].reshape(NY * ROWS, ref.shape[-1]) for b in stage_blocks(stage)], axis=0)

    own_block = [at_z(stage_offset(stage, col // 2)) for stage in range(STAGES)]
    own_half = pl.ds(2 * (col % 2), 2)

    def phase_b(stage):
        for quarter in range(4):
            grad_wait(stage_offset(stage, quarter))
        partial = dot(stage_rows(ga, stage), w_out[:, :HEAD], ((1,), (1,)))
        partial = (partial + dot(stage_rows(gb, stage), w_out[:, HEAD:], ((1,), (1,)))).astype(BF16)
        xs[stage] = partial.reshape(NC, 2, ROWS, partial.shape[-1])
        for r in col_offsets:
            send(xs.at[stage, other_col(r)], xr.at[stage, r], x_s.at[stage, r], x_r.at[stage, r], dev_c(r))

    def phase_c(stage):
        total = xs[stage, col].astype(F32)
        for r in col_offsets[::-1]:
            arrived(xr.at[stage, r], x_s.at[stage, r], x_r.at[stage, r])
            total = total + xr[stage, r].astype(F32)
        block = own_block[stage]
        own = pre[block, own_half].astype(F32)
        hid[block, own_half] = (total * gelu_grad(own)).astype(BF16)
        piece = hid.at[block, own_half]
        for r in col_offsets:
            send(piece, piece, h_s.at[stage, r], h_r.at[stage, r], dev_c(r))

    def phase_d(stage):
        for r in col_offsets[::-1]:
            source = source_col(r)
            piece = hid.at[at_z(stage_offset(stage, source // 2)), pl.ds(2 * (source % 2), 2)]
            arrived(piece, h_s.at[stage, r], h_r.at[stage, r])
        partial = dot(stage_rows(hid, stage), w_in[...], ((1,), (1,)))
        part[stage] = partial.reshape(4, NY, ROWS, partial.shape[-1])
        for quarter in (3, 0, 2, 1):
            for d in (2, 1, 3):
                slot = NY * quarter + d
                ys[stage, slot] = part[stage, quarter, at_y(d)].astype(BF16)
                send(ys.at[stage, slot], yr.at[stage, slot], y_s.at[stage, slot], y_r.at[stage, slot], dev_y(d))

    def phase_e(stage):
        for quarter in (3, 0, 2, 1):
            offset = stage_offset(stage, quarter)
            total = part[stage, quarter, y]
            for d in (1, 3, 2):
                slot = NY * quarter + d
                arrived(yr.at[stage, slot], y_s.at[stage, slot], y_r.at[stage, slot])
                total = total + yr[stage, slot].astype(F32)
            seen = slot_of(back(offset))
            zs[seen] = total.astype(BF16)
            if offset:
                send(zs.at[seen], zr.at[seen], z_s.at[seen], z_r.at[seen], dev_z(offset))

    for load in grad_loads:
        load.wait()
    grad_start()
    pre_load.wait()
    own_pre = pre.at[pl.ds(2 * col, 2)]
    for r in col_offsets:
        send(own_pre, own_pre, pre_s.at[r], pre_r.at[r], dev_c(r))
    weight_loads = [local(w_out_hbm, w_out, 4), local(w_in_hbm, w_in, 5)]

    def start_inputs():
        for load in inp_loads:
            load.wait()
        inp_start()

    def wait_preact():
        for r in col_offsets:
            arrived(pre.at[pl.ds(2 * source_col(r), 2)], pre_s.at[r], pre_r.at[r])

    def wait_weights():
        for load in weight_loads:
            load.wait()

    def gelu_part(index):
        gelu_chunk(2 * index)
        gelu_chunk(2 * index + 1)

    def w_out_grad():
        for gathered, columns in ((ga, slice(0, HEAD)), (gb, slice(HEAD, None))):
            wog[:, columns] = dot(flat(act), flat(gathered), ((0,), (0,)))

    def w_in_grad():
        if ib is not None:
            for offset in range(-7, 9):
                inp_wait(offset)
            wig[INP_HEAD:] = dot(flat(ib), flat(hid), ((0,), (0,)))
        wig[:INP_HEAD] = dot(flat(ia), flat(hid), ((0,), (0,)))

    for step, *index in (
        (grad_rest, 1), (grad_head, 0), (wait_weights,), (grad_rest, 2), (grad_head, 1), (start_inputs,),
        (phase_b, 0), (wait_preact,), (gelu_part, 0), (gelu_part, 1), (grad_rest, 3), (grad_head, 2), (phase_b, 1),
        (phase_c, 0), (inp_rest, 1), (inp_head, 0), (gelu_part, 2), (gelu_part, 3), (grad_rest, 4), (grad_head, 3),
        (phase_b, 2), (phase_c, 1), (phase_d, 0), (inp_rest, 2), (inp_head, 1), (grad_head, 4), (phase_b, 3),
        (phase_c, 2), (phase_d, 1), (phase_e, 0), (inp_rest, 3), (inp_head, 2), (w_out_grad,), (phase_c, 3),
        (phase_d, 2), (phase_e, 1), (inp_rest, 4), (inp_head, 3), (phase_d, 3), (phase_e, 2), (inp_head, 4),
        (phase_e, 3), (w_in_grad,),
    ):
        step(*index)

    total = zs[slot_of(0)].astype(F32)
    for offset in (1, -1, 2, -2, 3, -3, 4, -4, 5, -5, 6, -6, 7, -7, 8):
        seen = slot_of(offset)
        arrived(zr.at[seen], z_s.at[seen], z_r.at[seen])
        total = total + zr[seen].astype(F32)
    in_grad_ref[...] = total.astype(BF16)
    for copy in sends:
        copy.wait_send()


def body(inputs, out_grad, preact, w_in, w_out):
    width, hidden = w_in.shape
    dma = pltpu.SemaphoreType.DMA
    any_space = pl.BlockSpec(memory_space=pl.ANY)
    gather_sems = [dma((size,)) for size in (NY, NY, 16, 16, 16, 16, 16 * NY, 16 * NY)]
    pairs = [(NC,), (STAGES, NC), (STAGES, NC), (STAGES, 4 * NY), (16,)]
    return pl.pallas_call(
        kernel,
        name="mlp_backward",
        out_shape=(
            pltpu.VMEM((ROWS, width), BF16),
            pltpu.VMEM((width, hidden), F32),
            pltpu.VMEM((hidden, width), F32),
        ),
        in_specs=[any_space] * 5,
        out_specs=(pl.BlockSpec(memory_space=pltpu.VMEM),) * 3,
        scratch_shapes=[
            pltpu.VMEM((NZ, NY, ROWS, HEAD), BF16),
            pltpu.VMEM((NZ, NY, ROWS, width - HEAD), BF16),
            pltpu.VMEM((NZ, NY, ROWS, INP_HEAD), BF16),
            pltpu.VMEM((NZ, NY, ROWS, width - INP_HEAD), BF16) if INP_HEAD < width else None,
            pltpu.VMEM((NZ, NY, ROWS, hidden), BF16),
            pltpu.VMEM((NZ, NY, ROWS, hidden), BF16),
            pltpu.VMEM((NZ, NY, ROWS, hidden), BF16),
            pltpu.VMEM((width, hidden), BF16),
            pltpu.VMEM((hidden, width), BF16),
            pltpu.VMEM((STAGES, NC, 2, ROWS, hidden), BF16),
            pltpu.VMEM((STAGES, NC, 2, ROWS, hidden), BF16),
            pltpu.VMEM((STAGES, 4, NY, ROWS, width), F32),
            pltpu.VMEM((STAGES, 4 * NY, ROWS, width), BF16),
            pltpu.VMEM((STAGES, 4 * NY, ROWS, width), BF16),
            pltpu.VMEM((16, ROWS, width), BF16),
            pltpu.VMEM((16, ROWS, width), BF16),
            dma((7,)),
            gather_sems,
            gather_sems,
        ]
        + [dma(shape) for shape in pairs for _ in range(2)],
        compiler_params=pltpu.CompilerParams(collective_id=0, has_side_effects=True, vmem_limit_bytes=60 << 20),
    )(out_grad, inputs, preact.reshape(2, NY, ROWS, hidden), w_in, w_out)


def solution(mesh):
    placed = (
        P("wide", "col"),
        P("wide", "col"),
        P("col", "wide"),
        P("col", "wide"),
        P("wide", "col"),
    )
    return jax.shard_map(
        body,
        mesh=mesh,
        in_specs=placed,
        out_specs=(P("wide", "col"), P("col", "wide"), P("wide", "col")),
        check_vma=False,
    )
```

```python
import functools
import math

import jax
import jax.numpy as jnp
from jax import lax
from jax.experimental import pallas as pl
from jax.experimental.pallas import tpu as pltpu
from jax.sharding import PartitionSpec as P

MESH = pl.DeviceIdType.MESH
NZ, NY, NC = 16, 4, 8
ROWS = 16
HEAD = 256
INP_HEAD = 384
INP_REACH = 2
STAGES = 4
BF16, F32 = jnp.bfloat16, jnp.float32


def normal_cdf(values):
    return 0.5 * (1.0 + lax.erf(values * (1.0 / math.sqrt(2.0))))


def gelu_grad(values):
    density = jnp.exp(-0.5 * values * values) * (1.0 / math.sqrt(2.0 * math.pi))
    return normal_cdf(values) + values * density


def dot(a, b, contract):
    return lax.dot_general(a, b, (contract, ((), ())), preferred_element_type=F32)


def stage_offset(stage, quarter):
    return -(2 * stage + 1) + quarter % 2 + (4 * stage + 2) * (quarter // 2)


def slot_of(offset):
    return offset + 7


def back(offset):
    return 8 if offset == 8 else -offset


def kernel(
    grad_hbm, inp_hbm, pre_hbm, w_in_hbm, w_out_hbm,
    in_grad_ref, wig, wog,
    ga, gb, ia, ib, pre, act, hid, w_in, w_out, xs, xr, part, ys, yr, zs, zr,
    local_sem,
    grad_sems, inp_sems, pre_s, pre_r, x_s, x_r, h_s, h_r, y_s, y_r, z_s, z_r,
):
    wide, col = lax.axis_index("wide"), lax.axis_index("col")
    z, y, x, core = wide // NY, wide % NY, col // 2, col % 2

    def at_z(offset):
        return (z + offset + NZ) % NZ

    def at_y(offset):
        return (y + offset) % NY

    def dev_z(offset):
        return (at_z(offset) * NY + y, col)

    def dev_y(offset):
        return (z * NY + at_y(offset), col)

    col_offsets = (4, 5, 2, 3, 6, 7, 1)

    def other_col(offset):
        return 2 * ((x + offset // 2) % 4) + (core + offset) % 2

    def dev_c(offset):
        return (wide, other_col(offset))

    def source_col(offset):
        return 2 * ((x + 4 - offset // 2) % 4) + (core + offset) % 2

    sends = []

    def send(src, dst, send_sem, recv_sem, device):
        copy = pltpu.make_async_remote_copy(
            src_ref=src, dst_ref=dst, send_sem=send_sem, recv_sem=recv_sem, device_id=device, device_id_type=MESH
        )
        copy.start()
        sends.append(copy)

    def arrived(dst, send_sem, recv_sem):
        pltpu.make_async_remote_copy(
            src_ref=dst, dst_ref=dst, send_sem=send_sem, recv_sem=recv_sem, device_id=dev_y(1), device_id_type=MESH
        ).wait_recv()

    def local(src, dst, index):
        copy = pltpu.make_async_copy(src, dst, local_sem.at[index])
        copy.start()
        return copy

    grad_loads = [
        local(grad_hbm.at[:, HEAD:], gb.at[z, y], 0),
        local(grad_hbm.at[:, :HEAD], ga.at[z, y], 1),
    ]
    pre_load = local(pre_hbm, pre.at[pl.ds(2 * col, 2)], 2)
    inp_loads = [local(inp_hbm.at[:, INP_HEAD:], ib.at[z, y], 3)] if INP_HEAD < inp_hbm.shape[1] else []
    inp_loads.append(local(inp_hbm.at[:, :INP_HEAD], ia.at[z, y], 6))

    barrier = pltpu.get_barrier_semaphore()
    greeted = [dev_z(d) for d in (1, -1, 2, -2)] + [dev_y(d) for d in (1, 2, 3)] + [dev_c(r) for r in col_offsets]
    for other in greeted:
        pl.semaphore_signal(barrier, inc=1, device_id=other, device_id_type=MESH)
    pl.semaphore_wait(barrier, len(greeted))

    def gather(head, rest, sems, reach):
        hy_s, hy_r, hz_s, hz_r, rz_s, rz_r, ry_s, ry_r = sems

        def head_block(offset):
            return head.at[at_z(offset)], hz_s, hz_r

        def rest_block(offset):
            return rest.at[at_z(offset), y], rz_s, rz_r

        def z_pass(part, offset, hop):
            seen = slot_of(offset - hop)
            block, send_sem, recv_sem = part(offset)
            send(block, block, send_sem.at[seen], recv_sem.at[seen], dev_z(hop))

        def z_wait(part, offset):
            block, send_sem, recv_sem = part(offset)
            arrived(block, send_sem.at[slot_of(offset)], recv_sem.at[slot_of(offset)])

        def y_pass(offset):
            block = rest.at[at_z(offset), y]
            for d in (2, 1, 3):
                slot = NY * slot_of(offset) + d
                send(block, block, ry_s.at[slot], ry_r.at[slot], dev_y(d))

        def y_wait(offset):
            for d in (1, 2, 3):
                slot = NY * slot_of(offset) + d
                arrived(rest.at[at_z(offset), at_y(NY - d)], ry_s.at[slot], ry_r.at[slot])

        def z_start(part):
            for hop in range(reach, 0, -1):
                z_pass(part, 0, hop)
                z_pass(part, 0, -hop)

        def z_step(part, step, then):
            waiting = []
            for back_off in range(reach):
                for way in (1, -1):
                    offset = way * (reach * step - back_off)
                    if offset == -8:
                        continue
                    z_wait(part, offset)
                    if back_off == 0 and reach * step < 8:
                        for hop in range(reach, 0, -1):
                            if offset + hop * way != -8:
                                z_pass(part, offset, -hop * way)
                    waiting.append(offset)
                    if back_off or way < 0 or reach * step == 8:
                        for passed in waiting:
                            then(passed)
                        waiting = []

        def start():
            if rest is not None:
                z_start(rest_block)
            block = head.at[z, y]
            for d in (2, 1, 3):
                send(block, block, hy_s.at[d], hy_r.at[d], dev_y(d))
            if rest is not None:
                y_pass(0)

        def rest_step(step):
            z_step(rest_block, step, y_pass)

        def head_step(step):
            if step == 0:
                for d in (1, 2, 3):
                    arrived(head.at[z, at_y(NY - d)], hy_s.at[d], hy_r.at[d])
                z_start(head_block)
            else:
                z_step(head_block, step, lambda offset: None)

        return start, rest_step, head_step, y_wait

    grad_start, grad_rest, grad_head, grad_wait = gather(ga, gb, grad_sems, 2)
    inp_start, inp_rest, inp_head, inp_wait = gather(ia, ib, inp_sems, INP_REACH)

    def flat(ref):
        return ref[...].reshape(NZ * NY * ROWS, ref.shape[-1])

    def gelu_chunk(index):
        values = pre[pl.ds(2 * index, 2)].astype(F32)
        act[pl.ds(2 * index, 2)] = (values * normal_cdf(values)).astype(BF16)

    def stage_blocks(stage):
        return [at_z(stage_offset(stage, quarter)) for quarter in range(4)]

    def stage_rows(ref, stage):
        return jnp.concatenate([ref[b].reshape(NY * ROWS, ref.shape[-1]) for b in stage_blocks(stage)], axis=0)

    own_block = [at_z(stage_offset(stage, col // 2)) for stage in range(STAGES)]
    own_half = pl.ds(2 * (col % 2), 2)

    def phase_b(stage):
        for quarter in range(4):
            grad_wait(stage_offset(stage, quarter))
        partial = dot(stage_rows(ga, stage), w_out[:, :HEAD], ((1,), (1,)))
        partial = (partial + dot(stage_rows(gb, stage), w_out[:, HEAD:], ((1,), (1,)))).astype(BF16)
        xs[stage] = partial.reshape(NC, 2, ROWS, partial.shape[-1])
        for r in col_offsets:
            send(xs.at[stage, other_col(r)], xr.at[stage, r], x_s.at[stage, r], x_r.at[stage, r], dev_c(r))

    def phase_c(stage):
        total = xs[stage, col].astype(F32)
        for r in col_offsets[::-1]:
            arrived(xr.at[stage, r], x_s.at[stage, r], x_r.at[stage, r])
            total = total + xr[stage, r].astype(F32)
        block = own_block[stage]
        own = pre[block, own_half].astype(F32)
        hid[block, own_half] = (total * gelu_grad(own)).astype(BF16)
        piece = hid.at[block, own_half]
        for r in col_offsets:
            send(piece, piece, h_s.at[stage, r], h_r.at[stage, r], dev_c(r))

    def phase_d(stage):
        for r in col_offsets[::-1]:
            source = source_col(r)
            piece = hid.at[at_z(stage_offset(stage, source // 2)), pl.ds(2 * (source % 2), 2)]
            arrived(piece, h_s.at[stage, r], h_r.at[stage, r])
        partial = dot(stage_rows(hid, stage), w_in[...], ((1,), (1,)))
        part[stage] = partial.reshape(4, NY, ROWS, partial.shape[-1])
        for quarter in (3, 0, 2, 1):
            for d in (2, 1, 3):
                slot = NY * quarter + d
                ys[stage, slot] = part[stage, quarter, at_y(d)].astype(BF16)
                send(ys.at[stage, slot], yr.at[stage, slot], y_s.at[stage, slot], y_r.at[stage, slot], dev_y(d))

    def phase_e(stage):
        for quarter in (3, 0, 2, 1):
            offset = stage_offset(stage, quarter)
            total = part[stage, quarter, y]
            for d in (2, 1, 3):
                slot = NY * quarter + d
                arrived(yr.at[stage, slot], y_s.at[stage, slot], y_r.at[stage, slot])
                total = total + yr[stage, slot].astype(F32)
            seen = slot_of(back(offset))
            zs[seen] = total.astype(BF16)
            if offset:
                send(zs.at[seen], zr.at[seen], z_s.at[seen], z_r.at[seen], dev_z(offset))

    for load in grad_loads:
        load.wait()
    grad_start()
    pre_load.wait()
    own_pre = pre.at[pl.ds(2 * col, 2)]
    for r in col_offsets:
        send(own_pre, own_pre, pre_s.at[r], pre_r.at[r], dev_c(r))
    weight_loads = [local(w_out_hbm, w_out, 4), local(w_in_hbm, w_in, 5)]

    def start_inputs():
        for load in inp_loads:
            load.wait()
        inp_start()

    def wait_preact():
        for r in col_offsets:
            arrived(pre.at[pl.ds(2 * source_col(r), 2)], pre_s.at[r], pre_r.at[r])

    def wait_weights():
        for load in weight_loads:
            load.wait()

    def gelu_part(index):
        gelu_chunk(2 * index)
        gelu_chunk(2 * index + 1)

    def w_out_grad():
        for gathered, columns in ((ga, slice(0, HEAD)), (gb, slice(HEAD, None))):
            wog[:, columns] = dot(flat(act), flat(gathered), ((0,), (0,)))

    def w_in_grad():
        if ib is not None:
            for offset in range(-7, 9):
                inp_wait(offset)
            wig[INP_HEAD:] = dot(flat(ib), flat(hid), ((0,), (0,)))
        wig[:INP_HEAD] = dot(flat(ia), flat(hid), ((0,), (0,)))

    for step, *index in (
        (grad_rest, 1), (grad_head, 0), (wait_weights,), (grad_rest, 2), (grad_head, 1), (start_inputs,),
        (phase_b, 0), (wait_preact,), (gelu_part, 0), (gelu_part, 1), (grad_rest, 3), (grad_head, 2), (phase_b, 1),
        (phase_c, 0), (inp_rest, 1), (inp_head, 0), (gelu_part, 2), (gelu_part, 3), (grad_rest, 4), (grad_head, 3),
        (phase_b, 2), (phase_c, 1), (phase_d, 0), (inp_rest, 2), (inp_head, 1), (grad_head, 4), (phase_b, 3),
        (phase_c, 2), (phase_d, 1), (phase_e, 0), (inp_rest, 3), (inp_head, 2), (w_out_grad,), (phase_c, 3),
        (phase_d, 2), (phase_e, 1), (inp_rest, 4), (inp_head, 3), (phase_d, 3), (phase_e, 2), (inp_head, 4),
        (phase_e, 3), (w_in_grad,),
    ):
        step(*index)

    total = zs[slot_of(0)].astype(F32)
    for offset in (1, -1, 2, -2, 3, -3, 4, -4, 5, -5, 6, -6, 7, -7, 8):
        seen = slot_of(offset)
        arrived(zr.at[seen], z_s.at[seen], z_r.at[seen])
        total = total + zr[seen].astype(F32)
    in_grad_ref[...] = total.astype(BF16)
    for copy in sends:
        copy.wait_send()


def body(inputs, out_grad, preact, w_in, w_out):
    width, hidden = w_in.shape
    dma = pltpu.SemaphoreType.DMA
    any_space = pl.BlockSpec(memory_space=pl.ANY)
    gather_sems = [dma((size,)) for size in (NY, NY, 16, 16, 16, 16, 16 * NY, 16 * NY)]
    pairs = [(NC,), (STAGES, NC), (STAGES, NC), (STAGES, 4 * NY), (16,)]
    return pl.pallas_call(
        kernel,
        name="mlp_backward",
        out_shape=(
            pltpu.VMEM((ROWS, width), BF16),
            pltpu.VMEM((width, hidden), F32),
            pltpu.VMEM((hidden, width), F32),
        ),
        in_specs=[any_space] * 5,
        out_specs=(pl.BlockSpec(memory_space=pltpu.VMEM),) * 3,
        scratch_shapes=[
            pltpu.VMEM((NZ, NY, ROWS, HEAD), BF16),
            pltpu.VMEM((NZ, NY, ROWS, width - HEAD), BF16),
            pltpu.VMEM((NZ, NY, ROWS, INP_HEAD), BF16),
            pltpu.VMEM((NZ, NY, ROWS, width - INP_HEAD), BF16) if INP_HEAD < width else None,
            pltpu.VMEM((NZ, NY, ROWS, hidden), BF16),
            pltpu.VMEM((NZ, NY, ROWS, hidden), BF16),
            pltpu.VMEM((NZ, NY, ROWS, hidden), BF16),
            pltpu.VMEM((width, hidden), BF16),
            pltpu.VMEM((hidden, width), BF16),
            pltpu.VMEM((STAGES, NC, 2, ROWS, hidden), BF16),
            pltpu.VMEM((STAGES, NC, 2, ROWS, hidden), BF16),
            pltpu.VMEM((STAGES, 4, NY, ROWS, width), F32),
            pltpu.VMEM((STAGES, 4 * NY, ROWS, width), BF16),
            pltpu.VMEM((STAGES, 4 * NY, ROWS, width), BF16),
            pltpu.VMEM((16, ROWS, width), BF16),
            pltpu.VMEM((16, ROWS, width), BF16),
            dma((7,)),
            gather_sems,
            gather_sems,
        ]
        + [dma(shape) for shape in pairs for _ in range(2)],
        compiler_params=pltpu.CompilerParams(collective_id=0, has_side_effects=True, vmem_limit_bytes=60 << 20),
    )(out_grad, inputs, preact.reshape(2, NY, ROWS, hidden), w_in, w_out)


def solution(mesh):
    placed = (
        P("wide", "col"),
        P("wide", "col"),
        P("col", "wide"),
        P("col", "wide"),
        P("wide", "col"),
    )
    return jax.shard_map(
        body,
        mesh=mesh,
        in_specs=placed,
        out_specs=(P("wide", "col"), P("col", "wide"), P("wide", "col")),
        check_vma=False,
    )
```
